32 devices in a mesh: blk: 8 (over y, x, core), head: 4 (over z).
Axes of the slice: x: 2, y: 2, z: 4, core: 2. Of those that a mesh axis runs over, the one named last changes fastest.
Arguments:
- qkv: bfloat16 [4096, 8, 768], P(('blk', 'head')), may hold values from -40 to 40, as said below
- lambda_params: float32 [4, 128], replicated, may hold values from -0.4 to 0.4
- norm_gain: float32 [256], replicated, may hold values from 0.5 to 1.5
Outputs:
- mixed: bfloat16 [4096, 2048], P(('blk', 'head'))
The draws below stay inside these ranges and needn't reach their ends.
Inputs may be any that keep to these rules, and one draw needn't show every extreme that they name: `qkv`: entries of order one, some larger.
All inputs are finite; a program needn't handle non-finite values.
Results may differ from the reference program's by a relative error of at most 0.006.
Values may be sent and summed in bfloat16 or wider, within the bound.
A program may use at most 192 MiB of HBM per device.

```python
import math
import jax
import jax.numpy as jnp
from jax import lax

HEADS = 8
KEY_DIM = 128
VALUE_DIM = 256
TOK_DEV = 128
TOKENS = 4096
N_BLK = 8
N_HEAD = 4


def draw_qkv(key, part):
    key = jax.random.fold_in(key, 11)
    base_key = jax.random.fold_in(key, 0)
    lanes = 4 * KEY_DIM + VALUE_DIM
    shape = (TOKENS, HEADS, lanes)
    data = jnp.clip(jax.random.normal(base_key, shape, jnp.float32), -6.0, 6.0)
    return data.astype(jnp.bfloat16)


def setup_inputs(seed: int = 0) -> dict:
    arg_keys = jax.random.split(jax.random.key(seed), 4)
    return {
        "qkv": draw_qkv(jax.random.fold_in(arg_keys[3], 71), 0),
        "lambda_params": jnp.clip(jax.random.uniform(arg_keys[1], (4, KEY_DIM), jnp.float32, -0.4, 0.4), -0.4, 0.4),
        "norm_gain": jnp.clip(1.0 + 0.1 * jax.random.normal(arg_keys[2], (VALUE_DIM,), jnp.float32), 0.5, 1.5),
    }


lambda_init = 0.2
far_below = -1e+30

def reference(qkv, lambda_params, norm_gain):
    key_width = KEY_DIM
    block_rows = TOK_DEV * N_HEAD
    half_rows = block_rows // 2
    stored = jnp.arange(TOKENS, dtype=jnp.int32)
    owner = stored // block_rows
    within = stored % block_rows
    position = jnp.where(within < half_rows, owner * half_rows + within, (2 * N_BLK - 1 - owner) * half_rows + within - half_rows)
    lam_value = jnp.exp(jnp.sum(lambda_params[0] * lambda_params[1])) - jnp.exp(jnp.sum(lambda_params[2] * lambda_params[3])) + lambda_init
    score_scale = 1.0 / math.sqrt(KEY_DIM)

    def one_head(head):
        columns = lax.dynamic_index_in_dim(qkv, head, axis=1, keepdims=False)
        key_one = columns[:, 2 * key_width:3 * key_width]
        key_two = columns[:, 3 * key_width:4 * key_width]
        values_all = columns[:, 4 * key_width:]

        def one_block(block):
            begin = (block * block_rows).astype(jnp.int32)
            rows_here = lax.dynamic_slice_in_dim(columns, begin, block_rows, 0)
            query_pos = lax.dynamic_slice_in_dim(position, begin, block_rows, 0)
            visible = position[None, :] <= query_pos[:, None]

            def attend(queries, keys_all):
                scores = lax.dot_general(queries, keys_all, (((1,), (1,)), ((), ())), preferred_element_type=jnp.float32) * score_scale
                row_top = lax.optimization_barrier(jnp.max(jnp.where(visible, scores, far_below), axis=1, keepdims=True))
                expsum = jnp.where(visible, jnp.exp(scores - row_top), 0.0)
                product = jnp.dot(expsum.astype(jnp.bfloat16), values_all, preferred_element_type=jnp.float32)
                return product / lax.optimization_barrier(jnp.sum(expsum, axis=1, keepdims=True))
            out_one = attend(rows_here[:, 0:key_width], key_one)
            out_two = attend(rows_here[:, key_width:2 * key_width], key_two)
            difference = out_one - lam_value * out_two
            mean_square = lax.optimization_barrier(jnp.mean(difference * difference, axis=1, keepdims=True))
            normed = difference * lax.rsqrt(mean_square + 1e-05) * norm_gain * (1.0 - lambda_init)
            return normed.astype(jnp.bfloat16)
        return lax.map(one_block, jnp.arange(TOKENS // block_rows, dtype=jnp.int32))
    result = lax.map(one_head, jnp.arange(HEADS, dtype=jnp.int32))
    result = result.reshape(HEADS, TOKENS, VALUE_DIM)
    return jnp.transpose(result, (1, 0, 2)).reshape(TOKENS, HEADS * VALUE_DIM)
```

```python
import functools
import math

import jax
import jax.numpy as jnp
from jax import lax
from jax.experimental import pallas as pl
from jax.experimental.pallas import tpu as pltpu
from jax.sharding import PartitionSpec as P

lambda_init = 0.2
far_below = -1e30
MESH = pl.DeviceIdType.MESH


def flip(index, code):
    out = index
    bit = 1
    while bit <= code:
        if code & bit:
            out = out + (1 - 2 * ((index // bit) % 2)) * bit
        bit *= 2
    return out


def kernel(
    n_blk,
    n_head,
    x_ref,
    lam_ref,
    gain_ref,
    out_ref,
    kv,
    q,
    m_ref,
    l_ref,
    acc,
    obuf,
    send_kv,
    recv_kv,
    send_q,
    recv_q,
    send_o,
    recv_o,
):
    b = lax.axis_index("blk")
    h = lax.axis_index("head")
    tok = x_ref.shape[1]
    heads_here = q.shape[0]
    kd = lam_ref.shape[1]
    vd = gain_ref.shape[1]
    kvw = 2 * kd + vd
    rows_half = tok * n_head // 2
    subs = n_head // 2
    bits = [1 << i for i in range(n_blk.bit_length() - 1)]
    plane = bits[1:]
    orders = [
        (plane if hh % 2 == 0 else plane[::-1]) + bits[:1] for hh in range(heads_here)
    ]

    barrier = pltpu.get_barrier_semaphore()
    partners = [(b, flip(h, j)) for j in range(1, n_head)]
    partners += [(flip(b, bit), h) for bit in bits]
    for partner in partners:
        pl.semaphore_signal(barrier, inc=1, device_id=partner, device_id_type=MESH)
    pl.semaphore_wait(barrier, len(partners))

    def slot(hh, code, src):
        return kv.at[
            hh, src // subs, code, pl.ds(pl.multiple_of((src % subs) * tok, tok), tok), :
        ]

    def last_step(code, hh):
        return max(i for i, bit in enumerate(orders[hh]) if code & bit)

    def x_kv(head):
        return x_ref.at[head, :, pl.ds(2 * kd, kvw)]

    def head_copy(j, hh):
        dest = flip(h, j)
        return pltpu.make_async_remote_copy(
            src_ref=x_kv(dest * heads_here + hh),
            dst_ref=slot(hh, 0, h),
            send_sem=send_kv.at[0, j, hh],
            recv_sem=recv_kv.at[0, j, hh],
            device_id=(b, dest),
            device_id_type=MESH,
        )

    def q_rows(src):
        return q.at[:, pl.ds(pl.multiple_of(src * tok, tok), tok), :]

    def x_q(dest):
        return x_ref.at[pl.ds(dest * heads_here, heads_here), :, pl.ds(0, 2 * kd)]

    def q_copy(j):
        dest = flip(h, j)
        return pltpu.make_async_remote_copy(
            src_ref=x_q(dest),
            dst_ref=q_rows(h),
            send_sem=send_q.at[j],
            recv_sem=recv_q.at[j],
            device_id=(b, dest),
            device_id_type=MESH,
        )

    def own_copy(hh):
        return pltpu.make_async_copy(
            x_kv(h * heads_here + hh), slot(hh, 0, h), recv_kv.at[0, 0, hh]
        )

    def own_q():
        return pltpu.make_async_copy(x_q(h), q_rows(h), recv_q.at[0])

    def blk_copy(code, j, hh):
        bit = orders[hh][last_step(code, hh)]
        before = code ^ bit
        src = flip(h, j)
        if before == 0 and j == 0:
            source = x_kv(h * heads_here + hh)
        else:
            source = slot(hh, before, src)
        return pltpu.make_async_remote_copy(
            src_ref=source,
            dst_ref=slot(hh, code, src),
            send_sem=send_kv.at[code, j, hh],
            recv_sem=recv_kv.at[code, j, hh],
            device_id=(flip(b, bit), h),
            device_id_type=MESH,
        )

    arrived = set()

    def arrive(code, j, hh):
        if (code, j, hh) in arrived:
            return
        arrived.add((code, j, hh))
        if code == 0 and j == 0:
            pass
        elif code == 0:
            head_copy(j, hh).wait_recv()
        else:
            blk_copy(code, j, hh).wait_recv()
        first = 0 if code == 0 else last_step(code, hh) + 1
        for bit in orders[hh][first:]:
            blk_copy(code ^ bit, j, hh).start()

    def spread(step, j):
        for hh in range(heads_here):
            if step < 0:
                arrive(0, j, hh)
            else:
                for code in range(1, n_blk):
                    if last_step(code, hh) == step:
                        arrive(code, j, hh)

    steps = len(bits)

    for hh in range(heads_here):
        own_copy(hh).start()
    own_q().start()
    for hh in range(heads_here):
        head_copy(1, hh).start()
    for j in range(n_head - 1, 0, -1):
        q_copy(j).start()
    for j in range(2, n_head):
        for hh in range(heads_here):
            head_copy(j, hh).start()
    spread(-1, 0)

    m_ref[...] = jnp.full(m_ref.shape, far_below, jnp.float32)
    l_ref[...] = jnp.zeros(l_ref.shape, jnp.float32)
    acc[...] = jnp.zeros(acc.shape, jnp.float32)

    rate = math.log2(math.e) / math.sqrt(kd)
    chip = b // 2

    def unit(half, g, js):
        for hh in range(heads_here):
            for code in (2 * g, 2 * g + 1):
                for j in js:
                    arrive(code, j, hh)
        if g == 0:
            low = half
        else:
            top = 1 << (g.bit_length() - 1)
            later = 1 - (chip // top) % 2
            low = later + (1 - later) * 2 * half

        def one(hh, qt):
            rows = pl.ds(pl.multiple_of(qt * rows_half, rows_half), rows_half)
            values = kv[hh, half, 2 * g : 2 * g + 2, :, 2 * kd :].reshape(2 * rows_half, vd)
            for mp in range(2):
                queries = q[hh, rows, mp * kd : (mp + 1) * kd]
                keys = kv[hh, half, 2 * g : 2 * g + 2, :, mp * kd : (mp + 1) * kd]
                scores = lax.dot_general(
                    queries,
                    keys.reshape(2 * rows_half, kd),
                    (((1,), (1,)), ((), ())),
                    preferred_element_type=jnp.float32,
                )
                if g == 0:
                    row = lax.broadcasted_iota(jnp.int32, scores.shape, 0)
                    col = lax.broadcasted_iota(jnp.int32, scores.shape, 1)
                    sib = half + (1 - 2 * half) * (b % 2)
                    reach = qt * (1 - half) * 2 * rows_half
                    seen = (col <= row + reach) | (col >= 2 * rows_half - sib * rows_half)
                    scores = jnp.where(seen, scores, far_below)
                m_old = m_ref[hh, mp, rows]
                m_new = jnp.maximum(m_old, jnp.max(scores, axis=1, keepdims=True))
                weights = jnp.exp2((scores - m_new) * rate)
                factor = jnp.exp2((m_old - m_new) * rate)
                m_ref[hh, mp, rows] = m_new
                l_ref[hh, mp, rows] = l_ref[hh, mp, rows] * factor + jnp.sum(
                    weights, axis=1, keepdims=True
                )
                acc[hh, mp, rows] = acc[hh, mp, rows] * factor + jnp.dot(
                    weights.astype(jnp.bfloat16), values, preferred_element_type=jnp.float32
                )

        def over_rows(qt, carry):
            lax.fori_loop(0, heads_here, lambda hh, c: (one(hh, qt), c)[1], 0)
            return carry

        lax.fori_loop(low, 2, over_rows, 0)

    groups = n_blk // 2
    early = h // subs
    late = 1 - early
    near = list(range(subs))
    far = list(range(subs, n_head))

    for j in near[1:]:
        spread(-1, j)
    for j in near:
        for step in range(steps - 1):
            spread(step, j)
    for hh in range(heads_here):
        own_copy(hh).wait()
    own_q().wait()
    for j in range(1, n_head):
        q_copy(j).wait_recv()
    unit(early, 0, near)
    todo = [(step, far[0]) for step in range(-1, steps - 1)]
    for g in range(1, groups):
        if todo:
            spread(*todo.pop(0))
        unit(early, g, near)
    for item in todo:
        spread(*item)
    for j in far[1:]:
        spread(-1, j)
    unit(late, 0, far)
    for j in far[1:]:
        for step in range(steps - 1):
            spread(step, j)
    for g in range(1, groups):
        unit(late, g, far)

    lam = (
        jnp.exp(jnp.sum(lam_ref[0:1, :] * lam_ref[1:2, :], axis=1, keepdims=True))
        - jnp.exp(jnp.sum(lam_ref[2:3, :] * lam_ref[3:4, :], axis=1, keepdims=True))
        + lambda_init
    )
    gain = gain_ref[...] * (1.0 - lambda_init)

    def finish(src):
        rows = pl.ds(pl.multiple_of(src * tok, tok), tok)
        for hh in range(heads_here):
            one_out = acc[hh, 0, rows] * (1.0 / l_ref[hh, 0, rows])
            two_out = acc[hh, 1, rows] * (lam / l_ref[hh, 1, rows])
            difference = one_out - two_out
            mean_square = jnp.mean(difference * difference, axis=1, keepdims=True)
            obuf[rows, hh * vd : (hh + 1) * vd] = (
                difference * lax.rsqrt(mean_square + 1e-05) * gain
            ).astype(jnp.bfloat16)

    width = heads_here * vd

    def place(owner):
        return out_ref.at[:, pl.ds(pl.multiple_of(owner * width, width), width)]

    def out_rows(src):
        return obuf.at[pl.ds(pl.multiple_of(src * tok, tok), tok), :]

    def out_copy(j):
        dest = flip(h, j)
        return pltpu.make_async_remote_copy(
            src_ref=out_rows(dest),
            dst_ref=place(h),
            send_sem=send_o.at[j],
            recv_sem=recv_o.at[j],
            device_id=(b, dest),
            device_id_type=MESH,
        )

    for j in range(n_head - 1, 0, -1):
        finish(flip(h, j))
        out_copy(j).start()
    finish(h)
    own_out = pltpu.make_async_copy(out_rows(h), place(h), recv_o.at[0])
    own_out.start()
    own_out.wait()

    for j in range(1, n_head):
        q_copy(j).wait_send()
        for hh in range(heads_here):
            head_copy(j, hh).wait_send()
    for j in range(n_head):
        for hh in range(heads_here):
            for code in range(1, n_blk):
                blk_copy(code, j, hh).wait_send()
    for j in range(1, n_head):
        out_copy(j).wait()


def local(n_blk, n_head, qkv, lambda_params, norm_gain):
    tok, heads, lanes = qkv.shape
    kd = lambda_params.shape[1]
    vd = norm_gain.shape[0]
    heads_here = heads // n_head
    rows = tok * n_head
    by_head = jnp.transpose(qkv, (1, 0, 2))
    return pl.pallas_call(
        functools.partial(kernel, n_blk, n_head),
        out_shape=jax.ShapeDtypeStruct((tok, heads * vd), jnp.bfloat16),
        in_specs=[
            pl.BlockSpec(memory_space=pl.ANY),
            pl.BlockSpec(memory_space=pltpu.VMEM),
            pl.BlockSpec(memory_space=pltpu.VMEM),
        ],
        out_specs=pl.BlockSpec(memory_space=pl.ANY),
        scratch_shapes=[
            pltpu.VMEM((heads_here, 2, n_blk, rows // 2, 2 * kd + vd), jnp.bfloat16),
            pltpu.VMEM((heads_here, rows, 2 * kd), jnp.bfloat16),
            pltpu.VMEM((heads_here, 2, rows, 1), jnp.float32),
            pltpu.VMEM((heads_here, 2, rows, 1), jnp.float32),
            pltpu.VMEM((heads_here, 2, rows, vd), jnp.float32),
            pltpu.VMEM((rows, heads_here * vd), jnp.bfloat16),
            pltpu.SemaphoreType.DMA((n_blk, n_head, heads_here)),
            pltpu.SemaphoreType.DMA((n_blk, n_head, heads_here)),
            pltpu.SemaphoreType.DMA((n_head,)),
            pltpu.SemaphoreType.DMA((n_head,)),
            pltpu.SemaphoreType.DMA((n_head,)),
            pltpu.SemaphoreType.DMA((n_head,)),
        ],
        compiler_params=pltpu.CompilerParams(
            collective_id=0, has_side_effects=True, vmem_limit_bytes=56 * 1024 * 1024
        ),
    )(by_head, lambda_params, norm_gain.reshape(1, vd))


def solution(mesh):
    n_blk, n_head = mesh.shape["blk"], mesh.shape["head"]
    return jax.shard_map(
        functools.partial(local, n_blk, n_head),
        mesh=mesh,
        in_specs=(P(("blk", "head"), None, None), P(), P()),
        out_specs=P(("blk", "head"), None),
        check_vma=False,
    )
```

```python
import functools
import math

import jax
import jax.numpy as jnp
from jax import lax
from jax.experimental import pallas as pl
from jax.experimental.pallas import tpu as pltpu
from jax.sharding import PartitionSpec as P

lambda_init = 0.2
far_below = -1e30
MESH = pl.DeviceIdType.MESH


def flip(index, code):
    out = index
    bit = 1
    while bit <= code:
        if code & bit:
            out = out + (1 - 2 * ((index // bit) % 2)) * bit
        bit *= 2
    return out


def kernel(
    n_blk,
    n_head,
    x_ref,
    lam_ref,
    gain_ref,
    out_ref,
    kv,
    q,
    m_ref,
    l_ref,
    acc,
    obuf,
    send_kv,
    recv_kv,
    send_q,
    recv_q,
    send_o,
    recv_o,
):
    b = lax.axis_index("blk")
    h = lax.axis_index("head")
    tok = x_ref.shape[1]
    heads_here = q.shape[0]
    kd = lam_ref.shape[1]
    vd = gain_ref.shape[1]
    kvw = 2 * kd + vd
    rows_half = tok * n_head // 2
    subs = n_head // 2
    bits = [1 << i for i in range(n_blk.bit_length() - 1)]
    plane = bits[1:]
    orders = [plane + bits[:1], plane[::-1] + bits[:1]]

    barrier = pltpu.get_barrier_semaphore()
    partners = [(b, flip(h, j)) for j in range(1, n_head)]
    partners += [(flip(b, bit), h) for bit in bits]
    for partner in partners:
        pl.semaphore_signal(barrier, inc=1, device_id=partner, device_id_type=MESH)
    pl.semaphore_wait(barrier, len(partners))

    def slot(hh, code, src):
        return kv.at[
            hh, src // subs, code, pl.ds(pl.multiple_of((src % subs) * tok, tok), tok), :
        ]

    def last_step(code, way):
        return max(i for i, bit in enumerate(orders[way]) if code & bit)

    def x_kv(head):
        return x_ref.at[head, :, pl.ds(2 * kd, kvw)]

    def head_copy(j, hh):
        dest = flip(h, j)
        return pltpu.make_async_remote_copy(
            src_ref=x_kv(dest * heads_here + hh),
            dst_ref=slot(hh, 0, h),
            send_sem=send_kv.at[0, j, hh],
            recv_sem=recv_kv.at[0, j, hh],
            device_id=(b, dest),
            device_id_type=MESH,
        )

    def q_rows(src):
        return q.at[:, pl.ds(pl.multiple_of(src * tok, tok), tok), :]

    def x_q(dest):
        return x_ref.at[pl.ds(dest * heads_here, heads_here), :, pl.ds(0, 2 * kd)]

    def q_copy(j):
        dest = flip(h, j)
        return pltpu.make_async_remote_copy(
            src_ref=x_q(dest),
            dst_ref=q_rows(h),
            send_sem=send_q.at[j],
            recv_sem=recv_q.at[j],
            device_id=(b, dest),
            device_id_type=MESH,
        )

    def own_copy(hh):
        return pltpu.make_async_copy(
            x_kv(h * heads_here + hh), slot(hh, 0, h), recv_kv.at[0, 0, hh]
        )

    def own_q():
        return pltpu.make_async_copy(x_q(h), q_rows(h), recv_q.at[0])

    def blk_copy(code, j, hh):
        way = (hh + j) % 2
        bit = orders[way][last_step(code, way)]
        before = code ^ bit
        src = flip(h, j)
        if before == 0 and j == 0:
            source = x_kv(h * heads_here + hh)
        else:
            source = slot(hh, before, src)
        return pltpu.make_async_remote_copy(
            src_ref=source,
            dst_ref=slot(hh, code, src),
            send_sem=send_kv.at[code, j, hh],
            recv_sem=recv_kv.at[code, j, hh],
            device_id=(flip(b, bit), h),
            device_id_type=MESH,
        )

    steps = len(bits)
    near = list(range(subs))
    far = list(range(subs, n_head))
    heads = list(range(heads_here))

    def arrive(arrived, code, j, hh):
        if (code, j, hh) in arrived:
            return
        arrived.add((code, j, hh))
        way = (hh + j) % 2
        if code == 0 and j:
            head_copy(j, hh).wait_recv()
        elif code:
            blk_copy(code, j, hh).wait_recv()
        first = 0 if code == 0 else last_step(code, way) + 1
        for bit in orders[way][first:]:
            blk_copy(code ^ bit, j, hh).start()

    def spread(arrived, step, js, hhs):
        for j in js:
            for hh in hhs:
                if step < 0:
                    arrive(arrived, 0, j, hh)
                    continue
                for code in range(1, n_blk):
                    if last_step(code, (hh + j) % 2) == step:
                        arrive(arrived, code, j, hh)

    def inner(arrived, js, hhs, first=0):
        for step in range(first, steps - 1):
            spread(arrived, step, js, hhs)

    far_keys = [head_copy(j, hh) for hh in heads for j in far]
    far_queries = [q_copy(j) for j in far]
    queue_low = far_keys + far_queries
    queue_high = far_queries + far_keys
    third = len(queue_low) // 3
    cuts = [0, third + third // 2, 2 * third + third // 2, len(queue_low)]

    def send(queue, stage):
        for copy in queue[cuts[stage] : cuts[stage + 1]]:
            copy.start()

    for hh in heads:
        own_copy(hh).start()
    own_q().start()
    for j in near[1:]:
        for hh in heads:
            head_copy(j, hh).start()
    pl.when(h < subs)(functools.partial(send, queue_low, 0))
    pl.when(h >= subs)(functools.partial(send, queue_high, 0))
    for j in near[1:]:
        q_copy(j).start()
    sent_own = set()
    spread(sent_own, -1, [0], heads)

    m_ref[...] = jnp.full(m_ref.shape, far_below, jnp.float32)
    l_ref[...] = jnp.zeros(l_ref.shape, jnp.float32)
    acc[...] = jnp.zeros(acc.shape, jnp.float32)

    rate = math.log2(math.e) / math.sqrt(kd)
    chip = b // 2

    def one(half, g, hh, qt):
        rows = pl.ds(pl.multiple_of(qt * rows_half, rows_half), rows_half)
        values = kv[hh, half, pl.ds(2 * g, 2), :, 2 * kd :].reshape(2 * rows_half, vd)
        for mp in range(2):
            queries = q[hh, rows, mp * kd : (mp + 1) * kd]
            keys = kv[hh, half, pl.ds(2 * g, 2), :, mp * kd : (mp + 1) * kd]
            scores = lax.dot_general(
                queries,
                keys.reshape(2 * rows_half, kd),
                (((1,), (1,)), ((), ())),
                preferred_element_type=jnp.float32,
            )
            if isinstance(g, int) and g == 0:
                row = lax.broadcasted_iota(jnp.int32, scores.shape, 0)
                col = lax.broadcasted_iota(jnp.int32, scores.shape, 1)
                sib = half + (1 - 2 * half) * (b % 2)
                reach = qt * (1 - half) * 2 * rows_half
                seen = (col <= row + reach) | (col >= 2 * rows_half - sib * rows_half)
                scores = jnp.where(seen, scores, far_below)
            m_old = m_ref[hh, mp, rows]
            m_new = jnp.maximum(m_old, jnp.max(scores, axis=1, keepdims=True))
            weights = jnp.exp2((scores - m_new) * rate)
            factor = jnp.exp2((m_old - m_new) * rate)
            m_ref[hh, mp, rows] = m_new
            l_ref[hh, mp, rows] = l_ref[hh, mp, rows] * factor + jnp.sum(
                weights, axis=1, keepdims=True
            )
            acc[hh, mp, rows] = acc[hh, mp, rows] * factor + jnp.dot(
                weights.astype(jnp.bfloat16), values, preferred_element_type=jnp.float32
            )

    def lowest(half, g):
        if isinstance(g, int) and g == 0:
            return half
        later = 1 - (chip % 2)
        for top in [1 << i for i in range(1, groups.bit_length() - 1)]:
            later = jnp.where(g >= top, 1 - (chip // top) % 2, later)
        return later + (1 - later) * 2 * half

    groups = n_blk // 2
    chunks = [[0]]
    if groups <= 4:
        chunks += [[g] for g in range(1, groups)]
    else:
        chunks += [list(range(1, groups))]

    def work(arrived, half, chunk, hhs, js, qts):
        for hh in hhs:
            for g in chunk:
                for code in (2 * g, 2 * g + 1):
                    for j in js:
                        arrive(arrived, code, j, hh)

        def group(g):
            low = lowest(half, g)
            if qts == [1]:
                begin, end = jnp.maximum(low, 1), 2
            elif qts == [0]:
                begin, end = jnp.minimum(low, 1), 1
            else:
                begin, end = low, 2

            def row(qt, c):
                for hh in hhs:
                    one(half, g, hh, qt)
                return c

            lax.fori_loop(begin, end, row, 0)

        if len(chunk) == 1:
            group(chunk[0])
        else:
            lax.fori_loop(chunk[0], chunk[-1] + 1, lambda g, c: (group(g), c)[1], 0)

    lam = (
        jnp.exp(jnp.sum(lam_ref[0:1, :] * lam_ref[1:2, :], axis=1, keepdims=True))
        - jnp.exp(jnp.sum(lam_ref[2:3, :] * lam_ref[3:4, :], axis=1, keepdims=True))
        + lambda_init
    )
    gain = gain_ref[...] * (1.0 - lambda_init)

    def finish(hh, src):
        rows = pl.ds(pl.multiple_of(src * tok, tok), tok)
        one_out = acc[hh, 0, rows] * (1.0 / l_ref[hh, 0, rows])
        two_out = acc[hh, 1, rows] * (lam / l_ref[hh, 1, rows])
        difference = one_out - two_out
        mean_square = jnp.mean(difference * difference, axis=1, keepdims=True)
        obuf[rows, hh * vd : (hh + 1) * vd] = (
            difference * lax.rsqrt(mean_square + 1e-05) * gain
        ).astype(jnp.bfloat16)

    def place(owner, hh):
        return out_ref.at[:, pl.ds(pl.multiple_of((owner * heads_here + hh) * vd, vd), vd)]

    def out_rows(src, hh):
        return obuf.at[pl.ds(pl.multiple_of(src * tok, tok), tok), pl.ds(hh * vd, vd)]

    def out_copy(j, hh):
        dest = flip(h, j)
        return pltpu.make_async_remote_copy(
            src_ref=out_rows(dest, hh),
            dst_ref=place(h, hh),
            send_sem=send_o.at[j, hh],
            recv_sem=recv_o.at[j, hh],
            device_id=(b, dest),
            device_id_type=MESH,
        )

    def own_out(hh):
        return pltpu.make_async_copy(out_rows(h, hh), place(h, hh), recv_o.at[0, hh])

    def give(hh, js):
        for j in js:
            finish(hh, flip(h, j))
            (out_copy(j, hh) if j else own_out(hh)).start()

    def own_in():
        own_q().wait()
        for j in near[1:]:
            q_copy(j).wait_recv()
        for hh in heads:
            own_copy(hh).wait()

    def far_q_in():
        for j in far:
            q_copy(j).wait_recv()

    homeward = near[1:] + near[:1]

    def lower():
        got = set(sent_own)
        spread(got, -1, near[1:], heads)
        inner(got, near[:1], heads)
        spread(got, 0, near[1:], heads)
        far_q_in()
        send(queue_low, 1)
        inner(got, near[1:], heads, 1)
        own_in()
        work(got, 0, chunks[0], heads, near, [0, 1])
        for i, chunk in enumerate(chunks[1:]):
            work(got, 0, chunk, heads, near, [0, 1])
            if i == 0:
                spread(got, -1, far, heads[:1])
                send(queue_low, 2)
            if i == 1:
                spread(got, 0, far, heads[:1])
        inner(got, far, heads[:1])
        for hh in heads:
            rest = heads[hh + 1 : hh + 2]
            work(got, 1, chunks[0], [hh], far, [1])
            spread(got, -1, far, rest)
            for chunk in chunks[1:]:
                work(got, 1, chunk, [hh], far, [1])
            spread(got, 0, far, rest)
            give(hh, far)
            inner(got, far, rest, 1)
        for hh in heads:
            give(hh, homeward)

    def upper():
        got = set(sent_own)
        spread(got, -1, near[1:], heads)
        inner(got, near[:1], heads)
        spread(got, -1, far, heads[:1])
        send(queue_high, 1)
        spread(got, 0, near[1:], heads)
        spread(got, 0, far, heads[:1])
        inner(got, near[1:], heads, 1)
        own_in()
        work(got, 1, chunks[0], heads, near, [1])
        inner(got, far, heads[:1], 1)
        for chunk in chunks[1:]:
            work(got, 1, chunk, heads, near, [1])
        for hh in heads:
            rest = heads[hh + 1 : hh + 2]
            work(got, 0, chunks[0], [hh], far, [1])
            spread(got, -1, far, rest)
            if rest:
                send(queue_high, 2)
            for i, chunk in enumerate(chunks[1:]):
                work(got, 0, chunk, [hh], far, [1])
                if i == 0:
                    spread(got, 0, far, rest)
            inner(got, far, rest, 1)
        far_q_in()
        for hh in heads:
            for chunk in chunks:
                work(got, 0, chunk, [hh], far, [0])
            give(hh, far)
        for hh in heads:
            give(hh, homeward)

    pl.when(h < subs)(lower)
    pl.when(h >= subs)(upper)

    for hh in range(heads_here):
        own_out(hh).wait()
    for j in range(1, n_head):
        q_copy(j).wait_send()
        for hh in range(heads_here):
            head_copy(j, hh).wait_send()
    for j in range(n_head):
        for hh in range(heads_here):
            for code in range(1, n_blk):
                blk_copy(code, j, hh).wait_send()
    for j in range(1, n_head):
        for hh in range(heads_here):
            out_copy(j, hh).wait()


def local(n_blk, n_head, qkv, lambda_params, norm_gain):
    tok, heads, lanes = qkv.shape
    kd = lambda_params.shape[1]
    vd = norm_gain.shape[0]
    heads_here = heads // n_head
    rows = tok * n_head
    by_head = jnp.transpose(qkv, (1, 0, 2))
    return pl.pallas_call(
        functools.partial(kernel, n_blk, n_head),
        out_shape=jax.ShapeDtypeStruct((tok, heads * vd), jnp.bfloat16),
        in_specs=[
            pl.BlockSpec(memory_space=pl.ANY),
            pl.BlockSpec(memory_space=pltpu.VMEM),
            pl.BlockSpec(memory_space=pltpu.VMEM),
        ],
        out_specs=pl.BlockSpec(memory_space=pl.ANY),
        scratch_shapes=[
            pltpu.VMEM((heads_here, 2, n_blk, rows // 2, 2 * kd + vd), jnp.bfloat16),
            pltpu.VMEM((heads_here, rows, 2 * kd), jnp.bfloat16),
            pltpu.VMEM((heads_here, 2, rows, 1), jnp.float32),
            pltpu.VMEM((heads_here, 2, rows, 1), jnp.float32),
            pltpu.VMEM((heads_here, 2, rows, vd), jnp.float32),
            pltpu.VMEM((rows, heads_here * vd), jnp.bfloat16),
            pltpu.SemaphoreType.DMA((n_blk, n_head, heads_here)),
            pltpu.SemaphoreType.DMA((n_blk, n_head, heads_here)),
            pltpu.SemaphoreType.DMA((n_head,)),
            pltpu.SemaphoreType.DMA((n_head,)),
            pltpu.SemaphoreType.DMA((n_head, heads_here)),
            pltpu.SemaphoreType.DMA((n_head, heads_here)),
        ],
        compiler_params=pltpu.CompilerParams(
            collective_id=0, has_side_effects=True, vmem_limit_bytes=56 * 1024 * 1024
        ),
    )(by_head, lambda_params, norm_gain.reshape(1, vd))


def solution(mesh):
    n_blk, n_head = mesh.shape["blk"], mesh.shape["head"]
    return jax.shard_map(
        functools.partial(local, n_blk, n_head),
        mesh=mesh,
        in_specs=(P(("blk", "head"), None, None), P(), P()),
        out_specs=P(("blk", "head"), None),
        check_vma=False,
    )
```

```python
import functools
import math

import jax
import jax.numpy as jnp
from jax import lax
from jax.experimental import pallas as pl
from jax.experimental.pallas import tpu as pltpu
from jax.sharding import PartitionSpec as P

lambda_init = 0.2
far_below = -1e30
MESH = pl.DeviceIdType.MESH


def flip(index, code):
    out = index
    bit = 1
    while bit <= code:
        if code & bit:
            out = out + (1 - 2 * ((index // bit) % 2)) * bit
        bit *= 2
    return out


def kernel(
    n_blk,
    n_head,
    x_ref,
    lam_ref,
    gain_ref,
    out_ref,
    kv,
    q,
    m_ref,
    l_ref,
    acc,
    obuf,
    send_kv,
    recv_kv,
    send_q,
    recv_q,
    send_o,
    recv_o,
):
    b = lax.axis_index("blk")
    h = lax.axis_index("head")
    tok = x_ref.shape[1]
    heads_here = q.shape[0]
    kd = lam_ref.shape[1]
    vd = gain_ref.shape[1]
    kvw = 2 * kd + vd
    rows_half = tok * n_head // 2
    subs = n_head // 2
    bits = [1 << i for i in range(n_blk.bit_length() - 1)]
    plane = bits[1:]
    orders = [plane + bits[:1], plane[::-1] + bits[:1]]

    barrier = pltpu.get_barrier_semaphore()
    partners = [(b, flip(h, j)) for j in range(1, n_head)]
    partners += [(flip(b, bit), h) for bit in bits]
    for partner in partners:
        pl.semaphore_signal(barrier, inc=1, device_id=partner, device_id_type=MESH)
    pl.semaphore_wait(barrier, len(partners))

    def slot(hh, code, src):
        return kv.at[
            hh, src // subs, code, pl.ds(pl.multiple_of((src % subs) * tok, tok), tok), :
        ]

    def last_step(code, way):
        return max(i for i, bit in enumerate(orders[way]) if code & bit)

    def x_kv(head):
        return x_ref.at[head, :, pl.ds(2 * kd, kvw)]

    def head_copy(j, hh):
        dest = flip(h, j)
        return pltpu.make_async_remote_copy(
            src_ref=x_kv(dest * heads_here + hh),
            dst_ref=slot(hh, 0, h),
            send_sem=send_kv.at[0, j, hh],
            recv_sem=recv_kv.at[0, j, hh],
            device_id=(b, dest),
            device_id_type=MESH,
        )

    def q_rows(src):
        return q.at[:, pl.ds(pl.multiple_of(src * tok, tok), tok), :]

    def x_q(dest):
        return x_ref.at[pl.ds(dest * heads_here, heads_here), :, pl.ds(0, 2 * kd)]

    def q_copy(j):
        dest = flip(h, j)
        return pltpu.make_async_remote_copy(
            src_ref=x_q(dest),
            dst_ref=q_rows(h),
            send_sem=send_q.at[j],
            recv_sem=recv_q.at[j],
            device_id=(b, dest),
            device_id_type=MESH,
        )

    def own_copy(hh):
        return pltpu.make_async_copy(
            x_kv(h * heads_here + hh), slot(hh, 0, h), recv_kv.at[0, 0, hh]
        )

    def own_q():
        return pltpu.make_async_copy(x_q(h), q_rows(h), recv_q.at[0])

    def blk_copy(code, j, hh):
        way = (hh + j) % 2
        bit = orders[way][last_step(code, way)]
        before = code ^ bit
        src = flip(h, j)
        if before == 0 and j == 0:
            source = x_kv(h * heads_here + hh)
        else:
            source = slot(hh, before, src)
        return pltpu.make_async_remote_copy(
            src_ref=source,
            dst_ref=slot(hh, code, src),
            send_sem=send_kv.at[code, j, hh],
            recv_sem=recv_kv.at[code, j, hh],
            device_id=(flip(b, bit), h),
            device_id_type=MESH,
        )

    steps = len(bits)
    near = list(range(subs))
    far = list(range(subs, n_head))
    heads = list(range(heads_here))

    def arrive(arrived, code, j, hh):
        if (code, j, hh) in arrived:
            return
        arrived.add((code, j, hh))
        way = (hh + j) % 2
        if code == 0 and j:
            head_copy(j, hh).wait_recv()
        elif code:
            blk_copy(code, j, hh).wait_recv()
        first = 0 if code == 0 else last_step(code, way) + 1
        for bit in orders[way][first:]:
            blk_copy(code ^ bit, j, hh).start()

    def spread(arrived, step, js, hhs):
        for j in js:
            for hh in hhs:
                if step < 0:
                    arrive(arrived, 0, j, hh)
                    continue
                for code in range(1, n_blk):
                    if last_step(code, (hh + j) % 2) == step:
                        arrive(arrived, code, j, hh)

    def inner(arrived, js, hhs, first=0):
        for step in range(first, steps - 1):
            spread(arrived, step, js, hhs)

    far_keys = [head_copy(j, hh) for hh in heads for j in far]
    far_queries = [q_copy(j) for j in far]
    queue_low = far_keys + far_queries
    queue_high = far_queries + far_keys
    third = len(queue_low) // 3
    cuts = [0, 2 * third] + [len(queue_low)] * 2

    def send(queue, stage):
        for copy in queue[cuts[stage] : cuts[stage + 1]]:
            copy.start()

    for hh in heads:
        own_copy(hh).start()
    own_q().start()
    for j in near[1:]:
        for hh in heads:
            head_copy(j, hh).start()
    pl.when(h < subs)(functools.partial(send, queue_low, 0))
    pl.when(h >= subs)(functools.partial(send, queue_high, 0))
    for j in near[1:]:
        q_copy(j).start()
    sent_own = set()
    spread(sent_own, -1, [0], heads)

    m_ref[...] = jnp.full(m_ref.shape, far_below, jnp.float32)
    l_ref[...] = jnp.zeros(l_ref.shape, jnp.float32)
    acc[...] = jnp.zeros(acc.shape, jnp.float32)

    rate = math.log2(math.e) / math.sqrt(kd)
    chip = b // 2

    def one(half, g, hh, qt):
        rows = pl.ds(pl.multiple_of(qt * rows_half, rows_half), rows_half)
        values = kv[hh, half, pl.ds(2 * g, 2), :, 2 * kd :].reshape(2 * rows_half, vd)
        for mp in range(2):
            queries = q[hh, rows, mp * kd : (mp + 1) * kd]
            keys = kv[hh, half, pl.ds(2 * g, 2), :, mp * kd : (mp + 1) * kd]
            scores = lax.dot_general(
                queries,
                keys.reshape(2 * rows_half, kd),
                (((1,), (1,)), ((), ())),
                preferred_element_type=jnp.float32,
            )
            if isinstance(g, int) and g == 0:
                row = lax.broadcasted_iota(jnp.int32, scores.shape, 0)
                col = lax.broadcasted_iota(jnp.int32, scores.shape, 1)
                sib = half + (1 - 2 * half) * (b % 2)
                reach = qt * (1 - half) * 2 * rows_half
                seen = (col <= row + reach) | (col >= 2 * rows_half - sib * rows_half)
                scores = jnp.where(seen, scores, far_below)
            m_old = m_ref[hh, mp, rows]
            m_new = jnp.maximum(m_old, jnp.max(scores, axis=1, keepdims=True))
            weights = jnp.exp2((scores - m_new) * rate)
            factor = jnp.exp2((m_old - m_new) * rate)
            m_ref[hh, mp, rows] = m_new
            l_ref[hh, mp, rows] = l_ref[hh, mp, rows] * factor + jnp.sum(
                weights, axis=1, keepdims=True
            )
            acc[hh, mp, rows] = acc[hh, mp, rows] * factor + jnp.dot(
                weights.astype(jnp.bfloat16), values, preferred_element_type=jnp.float32
            )

    def lowest(half, g):
        if isinstance(g, int) and g == 0:
            return half
        later = 1 - (chip % 2)
        for top in [1 << i for i in range(1, groups.bit_length() - 1)]:
            later = jnp.where(g >= top, 1 - (chip // top) % 2, later)
        return later + (1 - later) * 2 * half

    groups = n_blk // 2
    chunks = [[0]]
    if groups <= 4:
        chunks += [[g] for g in range(1, groups)]
    else:
        chunks += [list(range(1, groups))]

    def work(arrived, half, chunk, hhs, js, qts):
        for hh in hhs:
            for g in chunk:
                for code in (2 * g, 2 * g + 1):
                    for j in js:
                        arrive(arrived, code, j, hh)

        def group(g):
            low = lowest(half, g)
            if qts == [1]:
                begin, end = jnp.maximum(low, 1), 2
            elif qts == [0]:
                begin, end = jnp.minimum(low, 1), 1
            else:
                begin, end = low, 2

            def row(qt, c):
                for hh in hhs:
                    one(half, g, hh, qt)
                return c

            lax.fori_loop(begin, end, row, 0)

        if len(chunk) == 1:
            group(chunk[0])
        else:
            lax.fori_loop(chunk[0], chunk[-1] + 1, lambda g, c: (group(g), c)[1], 0)

    lam = (
        jnp.exp(jnp.sum(lam_ref[0:1, :] * lam_ref[1:2, :], axis=1, keepdims=True))
        - jnp.exp(jnp.sum(lam_ref[2:3, :] * lam_ref[3:4, :], axis=1, keepdims=True))
        + lambda_init
    )
    gain = gain_ref[...] * (1.0 - lambda_init)

    def finish(hh, src):
        rows = pl.ds(pl.multiple_of(src * tok, tok), tok)
        one_out = acc[hh, 0, rows] * (1.0 / l_ref[hh, 0, rows])
        two_out = acc[hh, 1, rows] * (lam / l_ref[hh, 1, rows])
        difference = one_out - two_out
        mean_square = jnp.mean(difference * difference, axis=1, keepdims=True)
        obuf[rows, hh * vd : (hh + 1) * vd] = (
            difference * lax.rsqrt(mean_square + 1e-05) * gain
        ).astype(jnp.bfloat16)

    def place(owner, hh):
        return out_ref.at[:, pl.ds(pl.multiple_of((owner * heads_here + hh) * vd, vd), vd)]

    def out_rows(src, hh):
        return obuf.at[pl.ds(pl.multiple_of(src * tok, tok), tok), pl.ds(hh * vd, vd)]

    def out_copy(j, hh):
        dest = flip(h, j)
        return pltpu.make_async_remote_copy(
            src_ref=out_rows(dest, hh),
            dst_ref=place(h, hh),
            send_sem=send_o.at[j, hh],
            recv_sem=recv_o.at[j, hh],
            device_id=(b, dest),
            device_id_type=MESH,
        )

    def own_out(hh):
        return pltpu.make_async_copy(out_rows(h, hh), place(h, hh), recv_o.at[0, hh])

    def give(hh, js):
        for j in js:
            finish(hh, flip(h, j))
            (out_copy(j, hh) if j else own_out(hh)).start()

    def own_in():
        own_q().wait()
        for j in near[1:]:
            q_copy(j).wait_recv()
        for hh in heads:
            own_copy(hh).wait()

    def far_q_in():
        for j in far:
            q_copy(j).wait_recv()

    homeward = near[1:] + near[:1]

    def lower():
        got = set(sent_own)
        spread(got, -1, near[1:], heads)
        inner(got, near[:1], heads)
        spread(got, 0, near[1:], heads)
        far_q_in()
        send(queue_low, 1)
        inner(got, near[1:], heads, 1)
        own_in()
        work(got, 0, chunks[0], heads, near, [0, 1])
        for i, chunk in enumerate(chunks[1:]):
            work(got, 0, chunk, heads, near, [0, 1])
            if i == 0:
                spread(got, -1, far, heads[:1])
                send(queue_low, 2)
            if i == 1:
                spread(got, 0, far, heads[:1])
        inner(got, far, heads[:1])
        for hh in heads:
            rest = heads[hh + 1 : hh + 2]
            work(got, 1, chunks[0], [hh], far, [1])
            spread(got, -1, far, rest)
            for chunk in chunks[1:]:
                work(got, 1, chunk, [hh], far, [1])
            spread(got, 0, far, rest)
            give(hh, far)
            inner(got, far, rest, 1)
        for hh in heads:
            give(hh, homeward)

    def upper():
        got = set(sent_own)
        spread(got, -1, near[1:], heads)
        inner(got, near[:1], heads)
        spread(got, -1, far, heads[:1])
        send(queue_high, 1)
        spread(got, 0, near[1:], heads)
        spread(got, 0, far, heads[:1])
        inner(got, near[1:], heads, 1)
        own_in()
        work(got, 1, chunks[0], heads, near, [1])
        inner(got, far, heads[:1], 1)
        for chunk in chunks[1:]:
            work(got, 1, chunk, heads, near, [1])
        for hh in heads:
            rest = heads[hh + 1 : hh + 2]
            work(got, 0, chunks[0], [hh], far, [1])
            spread(got, -1, far, rest)
            if rest:
                send(queue_high, 2)
            for i, chunk in enumerate(chunks[1:]):
                work(got, 0, chunk, [hh], far, [1])
                if i == 0:
                    spread(got, 0, far, rest)
            inner(got, far, rest, 1)
        far_q_in()
        for hh in heads:
            for chunk in chunks:
                work(got, 0, chunk, [hh], far, [0])
            give(hh, far)
        for hh in heads:
            give(hh, homeward)

    pl.when(h < subs)(lower)
    pl.when(h >= subs)(upper)

    for hh in range(heads_here):
        own_out(hh).wait()
    for j in range(1, n_head):
        q_copy(j).wait_send()
        for hh in range(heads_here):
            head_copy(j, hh).wait_send()
    for j in range(n_head):
        for hh in range(heads_here):
            for code in range(1, n_blk):
                blk_copy(code, j, hh).wait_send()
    for j in range(1, n_head):
        for hh in range(heads_here):
            out_copy(j, hh).wait()


def local(n_blk, n_head, qkv, lambda_params, norm_gain):
    tok, heads, lanes = qkv.shape
    kd = lambda_params.shape[1]
    vd = norm_gain.shape[0]
    heads_here = heads // n_head
    rows = tok * n_head
    by_head = jnp.transpose(qkv, (1, 0, 2))
    return pl.pallas_call(
        functools.partial(kernel, n_blk, n_head),
        out_shape=jax.ShapeDtypeStruct((tok, heads * vd), jnp.bfloat16),
        in_specs=[
            pl.BlockSpec(memory_space=pl.ANY),
            pl.BlockSpec(memory_space=pltpu.VMEM),
            pl.BlockSpec(memory_space=pltpu.VMEM),
        ],
        out_specs=pl.BlockSpec(memory_space=pl.ANY),
        scratch_shapes=[
            pltpu.VMEM((heads_here, 2, n_blk, rows // 2, 2 * kd + vd), jnp.bfloat16),
            pltpu.VMEM((heads_here, rows, 2 * kd), jnp.bfloat16),
            pltpu.VMEM((heads_here, 2, rows, 1), jnp.float32),
            pltpu.VMEM((heads_here, 2, rows, 1), jnp.float32),
            pltpu.VMEM((heads_here, 2, rows, vd), jnp.float32),
            pltpu.VMEM((rows, heads_here * vd), jnp.bfloat16),
            pltpu.SemaphoreType.DMA((n_blk, n_head, heads_here)),
            pltpu.SemaphoreType.DMA((n_blk, n_head, heads_here)),
            pltpu.SemaphoreType.DMA((n_head,)),
            pltpu.SemaphoreType.DMA((n_head,)),
            pltpu.SemaphoreType.DMA((n_head, heads_here)),
            pltpu.SemaphoreType.DMA((n_head, heads_here)),
        ],
        compiler_params=pltpu.CompilerParams(
            collective_id=0, has_side_effects=True, vmem_limit_bytes=56 * 1024 * 1024
        ),
    )(by_head, lambda_params, norm_gain.reshape(1, vd))


def solution(mesh):
    n_blk, n_head = mesh.shape["blk"], mesh.shape["head"]
    return jax.shard_map(
        functools.partial(local, n_blk, n_head),
        mesh=mesh,
        in_specs=(P(("blk", "head"), None, None), P(), P()),
        out_specs=P(("blk", "head"), None),
        check_vma=False,
    )
```
